128 devices in a mesh: gx: 8 (over z, core), yz: 16 (over x, y).
Axes of the slice: x: 4, y: 4, z: 4, core: 2. Of those that a mesh axis runs over, the one named last changes fastest.
Arguments:
- residual: bfloat16 [512, 18432], P('yz', 'gx'), may hold values from -1000 to 1000
- norm_gain: float32 [18432], P('gx'), may hold values from 0.1 to 1.9
- query_weight: bfloat16 [18432, 12288], P('gx', 'yz'), may hold values from -1 to 1
- kv_weight: bfloat16 [18432, 512], P('gx', 'yz'), may hold values from -1 to 1
- cache: bfloat16 [512, 2048, 512], P(('gx', 'yz')), may hold values from -1000 to 1000
- ffn_hidden: bfloat16 [512, 36864], P('gx', 'yz'), may hold values from -3 to 3
- out_weight: bfloat16 [12288, 18432], P('yz', 'gx'), may hold values from -0.0546875 to 0.0546875
- down_weight: bfloat16 [36864, 18432], P('yz', 'gx'), may hold values from -0.03125 to 0.03125
Outputs:
- update: bfloat16 [512, 18432], P('yz', 'gx')
The draws below stay inside these ranges and needn't reach their ends.
All inputs are finite; a program needn't handle non-finite values.
Results may differ from the reference program's by a relative error of at most 0.02.
Values may be sent and summed in bfloat16 or wider, within the bound.
No kernel may reach another device: no remote copies, remote signals or barrier semaphores. Data moves between devices by JAX's collectives and lax.ppermute only.
A program may use at most 128 MiB of HBM per device.

```python
import jax
import jax.numpy as jnp
from jax import lax

D = 18432
HEADS = 48
HEAD = 256
FF = 36864
SEQ = 2048
ROWS = 512


alignment = 0.5


def shared_keys(key):
    return jax.random.truncated_normal(key, -4.0, 4.0, (D, HEAD), jnp.float32)


def draw_query_weight(key, part):
    common = shared_keys(key)
    key = jax.random.fold_in(key, 31)
    own_part = jax.random.truncated_normal(key, -4.0, 4.0, (D, HEADS, HEAD), jnp.float32)
    rest = (1.0 - alignment * alignment) ** 0.5
    mixed = (alignment * common[:, None, :] + rest * own_part) * D ** (-0.5)
    return mixed.reshape(D, HEADS * HEAD).astype(jnp.bfloat16)


def draw_kv_weight(key, part):
    common = shared_keys(key)
    key = jax.random.fold_in(key, 37)
    value_part = jax.random.truncated_normal(key, -4.0, 4.0, (D, HEAD), jnp.float32)
    return (jnp.concatenate([common, value_part], axis=1) * D ** (-0.5)).astype(jnp.bfloat16)


def draw_residual(key, part):
    key = jax.random.fold_in(key, 11)
    key_base, key_cols, key_rows = jax.random.split(key, 3)
    position = jnp.arange(D, dtype=jnp.float32) / D
    rise = jnp.exp(jnp.log(10.0) * position)
    col_scale = rise * jnp.exp(jax.random.uniform(key_cols, (D,), jnp.float32, 0.0, jnp.log(2.0)))
    row_scale = jnp.exp(jax.random.uniform(key_rows, (ROWS, 1), jnp.float32, 0.0, jnp.log(10.0)))
    base = jax.random.truncated_normal(key_base, -4.0, 4.0, (ROWS, D), jnp.float32)
    return (base * row_scale * col_scale[None, :]).astype(jnp.bfloat16)


def draw_cache(key, part):
    key = jax.random.fold_in(key, 23)
    key_keys, key_vals = jax.random.split(key, 2)
    keys_part = jax.random.truncated_normal(key_keys, -4.0, 4.0, (ROWS, SEQ, HEAD), jnp.float32)
    vals_part = jax.random.truncated_normal(key_vals, -4.0, 4.0, (ROWS, SEQ, HEAD), jnp.float32)
    return jnp.concatenate([keys_part, vals_part], axis=2).astype(jnp.bfloat16)


def spiked(values, stream_key, source, target, shards_of, factor):
    def block_of(dim):
        return (jnp.arange(values.shape[dim]) // (values.shape[dim] // shards_of)).reshape((-1,) + (1,) * (values.ndim - 1 - dim))

    one_side = jax.random.permutation(stream_key, shards_of)[block_of(target)]
    second = (block_of(target) + shards_of // 2) % shards_of
    return jnp.where((block_of(source) == one_side) | (block_of(source) == second), factor * values, values)


def levels(stream_key, extent, cuts, least, largest):
    level = 1.0
    for axis_at, shards_of in cuts:
        steps = jax.random.uniform(jax.random.fold_in(jax.random.fold_in(stream_key, 6), axis_at), (shards_of,), jnp.float32, least / len(cuts), largest / len(cuts))
        level = level * jnp.repeat(jnp.exp(steps), extent[axis_at] // shards_of).reshape((-1,) + (1,) * (len(extent) - 1 - axis_at))
    return level


def normal_values(own_key, extent, scale, bound, cuts=(), kind=jnp.bfloat16):
    gain = levels(own_key, extent, cuts, -0.22, 0.18) if cuts else 1.0
    values = jax.random.normal(own_key, extent, jnp.float32) * scale * gain
    return jnp.minimum(jnp.maximum(values, -bound), bound).astype(kind)


def bell_draw_with(key, dims, spread, bound, cuts, heavy, held_as=jnp.bfloat16):
    values = spread * jax.random.normal(key, dims, jnp.float32)
    if cuts:
        values = values * levels(key, dims, cuts, -0.22, 0.18)
    return jnp.clip(spiked(values, jax.random.fold_in(key, 3), *heavy), -bound, bound).astype(held_as)


def setup_inputs(seed: int = 0) -> dict:
    key_of = jax.random.split(jax.random.key(seed), 9)
    residual = draw_residual(jax.random.fold_in(key_of[8], 71), 0)
    norm_gain = jnp.clip(1.0 + 0.18 * jax.random.normal(key_of[1], (D,), jnp.float32), 0.1, 1.9)
    query_weight = draw_query_weight(jax.random.fold_in(key_of[8], 71), 0)
    kv_weight = draw_kv_weight(jax.random.fold_in(key_of[8], 71), 0)
    cache = draw_cache(jax.random.fold_in(key_of[8], 71), 0)
    ffn_hidden = bell_draw_with(key_of[5], (ROWS, FF), 0.5, 3.0, ((0, 8), (1, 16)), (1, 0, 16, 2.0))
    out_weight = normal_values(key_of[6], (HEADS * HEAD, D), (HEADS * HEAD) ** -0.5, 0.0546875, ((0, 16), (1, 8)))
    down_weight = normal_values(key_of[7], (FF, D), FF ** -0.5, 0.03125, ((0, 16), (1, 8)))
    return {"residual": residual, "norm_gain": norm_gain, "query_weight": query_weight, "kv_weight": kv_weight, "cache": cache, "ffn_hidden": ffn_hidden, "out_weight": out_weight, "down_weight": down_weight}


def layer_norm(residual, norm_gain):
    values = residual.astype(jnp.float32)
    mean = lax.optimization_barrier(jnp.mean(values, axis=1, keepdims=True))
    var = lax.optimization_barrier(jnp.mean(values * values, axis=1, keepdims=True)) - mean * mean
    return ((values - mean) * lax.rsqrt(var + 1e-05) * norm_gain[None, :]).astype(jnp.bfloat16)

def attend_row(inputs):
    query, past, fresh = inputs
    scale = HEAD ** (-0.5)
    scores = jnp.dot(query, past[:, :HEAD].T, preferred_element_type=jnp.float32) * scale
    own = jnp.dot(query, fresh[:HEAD], preferred_element_type=jnp.float32) * scale
    highest = jnp.maximum(lax.optimization_barrier(jnp.max(scores, axis=1)), own)
    e_past = jnp.exp(scores - highest[:, None])
    e_own = jnp.exp(own - highest)
    total = lax.optimization_barrier(jnp.sum(e_past, axis=1)) + e_own
    w_past = (e_past / total[:, None]).astype(jnp.bfloat16)
    w_own = (e_own / total).astype(jnp.bfloat16)
    result = jnp.dot(w_past, past[:, HEAD:], preferred_element_type=jnp.float32)
    result = result + w_own.astype(jnp.float32)[:, None] * fresh[HEAD:].astype(jnp.float32)[None, :]
    return result.astype(jnp.bfloat16).reshape(HEADS * HEAD)

def reference(residual, norm_gain, query_weight, kv_weight, cache, ffn_hidden, out_weight, down_weight):
    normed = layer_norm(residual, norm_gain)
    query = jnp.dot(normed, query_weight, preferred_element_type=jnp.float32).astype(jnp.bfloat16)
    fresh = jnp.dot(normed, kv_weight, preferred_element_type=jnp.float32).astype(jnp.bfloat16)
    heads = lax.map(attend_row, (query.reshape(ROWS, HEADS, HEAD), cache, fresh))
    update = jnp.dot(heads, out_weight, preferred_element_type=jnp.float32)
    update = update + jnp.dot(ffn_hidden, down_weight, preferred_element_type=jnp.float32)
    return update.astype(jnp.bfloat16)
```

```python
import jax
import jax.numpy as jnp
from jax import lax
from jax.sharding import Mesh, PartitionSpec as P

D = 18432
HEADS = 48
HEAD = 256
F32 = jnp.float32
BF16 = jnp.bfloat16
XY = ("x", "y")
ZC = ("z", "c")
ZXY = ("z", "x", "y")
SWAP = [(0, 1), (1, 0)]


def normalize(values, sums, squares, gain):
    mean = sums / D
    var = squares / D - mean * mean
    return ((values - mean[:, None]) * lax.rsqrt(var + 1e-05)[:, None] * gain[None, :]).astype(
        BF16
    )


def attend(query, fresh, cache):
    scale = HEAD ** (-0.5)
    scores = (
        jnp.einsum("rhd,rsd->rhs", query, cache[:, :, :HEAD], preferred_element_type=F32) * scale
    )
    own = jnp.einsum("rhd,rd->rh", query, fresh[:, :HEAD], preferred_element_type=F32) * scale
    highest = jnp.maximum(jnp.max(scores, axis=2), own)
    e_past = jnp.exp(scores - highest[:, :, None])
    e_own = jnp.exp(own - highest)
    total = jnp.sum(e_past, axis=2) + e_own
    w_past = (e_past / total[:, :, None]).astype(BF16)
    w_own = (e_own / total).astype(BF16)
    result = jnp.einsum("rhs,rsd->rhd", w_past, cache[:, :, HEAD:], preferred_element_type=F32)
    result = result + w_own.astype(F32)[:, :, None] * fresh[:, None, HEAD:].astype(F32)
    return result.astype(BF16)


def body(residual, norm_gain, query_weight, kv_weight, cache, ffn_hidden, out_weight, down_weight):
    core = lax.axis_index("c")
    query_cols = query_weight.shape[1]
    fresh_cols = kv_weight.shape[1]
    own_rows, width = residual.shape

    hidden = lax.all_gather(ffn_hidden, ZC, axis=0, tiled=True)

    values = residual.astype(F32)
    sums, squares = lax.psum((jnp.sum(values, axis=1), jnp.sum(values * values, axis=1)), ZC)
    normed = normalize(values, sums, squares, norm_gain)
    gathered = lax.all_to_all(
        jnp.broadcast_to(normed[None], (16, own_rows, width)), XY, 0, 0
    ).reshape(16 * own_rows, width)

    query_term = jnp.dot(gathered, query_weight, preferred_element_type=F32)
    fresh_term = jnp.dot(gathered, kv_weight, preferred_element_type=F32)
    terms = jnp.concatenate([query_term, fresh_term], axis=1).astype(BF16)
    cols = query_cols + fresh_cols
    split = terms.reshape(4, 2, 64, cols)
    mine = lax.dynamic_index_in_dim(split, core, 1, keepdims=False)
    theirs = lax.dynamic_index_in_dim(split, 1 - core, 1, keepdims=False)
    paired = (mine.astype(F32) + lax.ppermute(theirs, "c", SWAP).astype(F32)).astype(BF16)
    parts = lax.all_to_all(paired.reshape(64, 4, cols), ZXY, 0, 0)
    summed = jnp.sum(parts.reshape(4, 16, 4, cols).astype(F32), axis=0).astype(BF16)
    summed = summed.transpose(1, 0, 2)
    query = summed[:, :, :query_cols].reshape(4, HEADS, HEAD)
    fresh = summed[:, :, query_cols:].reshape(4, 2 * HEAD)

    attended = attend(query, fresh, cache).reshape(4, 16, query_cols).transpose(1, 0, 2)
    back = lax.all_to_all(
        jnp.broadcast_to(attended[None], (4, 16, 4, query_cols)).reshape(64, 4, query_cols),
        ZXY, 0, 0,
    ).reshape(4, 1, 64, query_cols)
    other = lax.ppermute(back, "c", SWAP)
    heads = jnp.where(
        core == 0, jnp.concatenate([back, other], axis=1), jnp.concatenate([other, back], axis=1)
    ).reshape(512, query_cols)

    ffn = jnp.dot(hidden, down_weight, preferred_element_type=F32)
    terms = (ffn + jnp.dot(heads, out_weight, preferred_element_type=F32)).astype(BF16)
    pieces = lax.all_to_all(terms.reshape(16, own_rows, width), XY, 0, 0)
    return jnp.sum(pieces.astype(F32), axis=0).astype(BF16)


def solution(mesh):
    fine = Mesh(mesh.devices.reshape(4, 2, 4, 4), ("z", "c", "x", "y"))
    placed = (
        P(XY, ZC),
        P(ZC),
        P(ZC, XY),
        P(ZC, XY),
        P(("z", "c", "x", "y"), None, None),
        P(ZC, XY),
        P(XY, ZC),
        P(XY, ZC),
    )
    return jax.shard_map(body, mesh=fine, in_specs=placed, out_specs=P(XY, ZC), check_vma=False)
```

```python
import functools

import jax
import jax.numpy as jnp
from jax import lax
from jax.experimental import pallas as pl
from jax.experimental.pallas import tpu as pltpu
from jax.sharding import Mesh, PartitionSpec as P

D = 18432
HEADS = 48
HEAD = 256
F32 = jnp.float32
BF16 = jnp.bfloat16
XY = ("x", "y")
ZC = ("z", "c")
ZXY = ("z", "x", "y")
SWAP = [(0, 1), (1, 0)]
WIDE = 58 << 20
NARROW = 8 << 20


def lower_rows(shape):
    return lax.broadcasted_iota(jnp.int32, shape, 1) < 4


def moments_kernel(residual_ref, out_ref):
    values = residual_ref[...].astype(F32)
    sums = jnp.sum(values, axis=1, keepdims=True)
    squares = jnp.sum(values * values, axis=1, keepdims=True)
    lanes = lax.broadcasted_iota(jnp.int32, out_ref.shape, 1)
    out_ref[...] = jnp.where(lanes < 64, sums, squares)


def row_moments(residual):
    return pl.pallas_call(
        moments_kernel,
        out_shape=jax.ShapeDtypeStruct((residual.shape[0], 128), F32),
        compiler_params=pltpu.CompilerParams(vmem_limit_bytes=NARROW),
        name="row_moments",
    )(residual)


def normalize_kernel(residual_ref, moments_ref, more_ref, gain_ref, out_ref):
    moments = moments_ref[...] + more_ref[...]
    mean = moments[:, 0:1] / D
    var = moments[:, 64:65] / D - mean * mean
    values = residual_ref[...].astype(F32)
    normed = ((values - mean) * lax.rsqrt(var + 1e-05) * gain_ref[...]).astype(BF16)
    for i in range(out_ref.shape[0]):
        out_ref[i] = normed


def normalize(residual, moments, more, gain):
    rows, width = residual.shape
    return pl.pallas_call(
        normalize_kernel,
        out_shape=jax.ShapeDtypeStruct((16, rows, width), BF16),
        compiler_params=pltpu.CompilerParams(vmem_limit_bytes=NARROW),
        name="normalize",
    )(residual, moments, more, gain)


def feed_kernel(own_ref, other_ref, weight_ref, out_ref):
    rows = own_ref.shape[0]
    weight = weight_ref[...]
    out_ref[:rows, :] = jnp.dot(own_ref[...], weight, preferred_element_type=F32)
    out_ref[rows:, :] = jnp.dot(other_ref[...], weight, preferred_element_type=F32)


def feed(own, other, weight):
    rows, depth = own.shape
    width = weight.shape[1]
    tile = 256
    whole = pl.BlockSpec((rows, depth), lambda i: (0, 0), pipeline_mode=pl.Buffered(1))
    return pl.pallas_call(
        feed_kernel,
        grid=(width // tile,),
        in_specs=[whole, whole, pl.BlockSpec((depth, tile), lambda i: (0, i))],
        out_specs=pl.BlockSpec((2 * rows, tile), lambda i: (0, i)),
        out_shape=jax.ShapeDtypeStruct((2 * rows, width), F32),
        compiler_params=pltpu.CompilerParams(vmem_limit_bytes=WIDE),
        cost_estimate=pl.CostEstimate(flops=1, bytes_accessed=1, transcendentals=0),
        name="feed",
    )(own, other, weight)


def project_kernel(x_ref, query_ref, fresh_ref, mine_ref, theirs_ref, slots_ref):
    core = lax.axis_index("c")
    step = pl.program_id(0)

    @pl.when(step < 3)
    def _():
        slots_ref[step] = jnp.dot(x_ref[...], query_ref[...], preferred_element_type=F32)

    @pl.when(step == 3)
    def _():
        fresh = jnp.dot(x_ref[...], fresh_ref[...], preferred_element_type=F32)
        fresh = jnp.concatenate([fresh, jnp.zeros_like(fresh)], axis=1)
        low = lower_rows((8, 8, HEAD))
        for block in range(8):
            z, c = block // 2, block % 2
            rows = slice(block * 64, block * 64 + 64)
            s = [slots_ref[h, rows, :] for h in range(3)] + [fresh[rows]]
            s = [v.reshape(8, 8, HEAD) for v in s]
            r = [pltpu.roll(v, 4, 1) for v in s]
            even = jnp.concatenate([jnp.where(low, s[0], r[1]), jnp.where(low, s[2], r[3])], axis=1)
            odd = jnp.concatenate([jnp.where(low, r[0], s[1]), jnp.where(low, r[2], s[3])], axis=1)

            def put(ref, z=z, even=even, odd=odd):
                ref[z, :, 0] = even.astype(BF16)
                ref[z, :, 1] = odd.astype(BF16)

            pl.when(core == c)(functools.partial(put, mine_ref))
            pl.when(core != c)(functools.partial(put, theirs_ref))


def project(x, query_weight, fresh_weight):
    rows, width = x.shape
    out = jax.ShapeDtypeStruct((4, 8, 2, 16, HEAD), BF16)
    return pl.pallas_call(
        project_kernel,
        grid=(4,),
        in_specs=[
            pl.BlockSpec((rows, width), lambda i: (0, 0), pipeline_mode=pl.Buffered(1)),
            pl.BlockSpec((width, HEAD), lambda i: (0, jnp.minimum(i, 2))),
            pl.BlockSpec(fresh_weight.shape, lambda i: (0, 0), pipeline_mode=pl.Buffered(1)),
        ],
        out_specs=[pl.BlockSpec(out.shape, lambda i: (0, 0, 0, 0, 0))] * 2,
        out_shape=[out, out],
        scratch_shapes=[pltpu.VMEM((3, rows, HEAD), F32)],
        compiler_params=pltpu.CompilerParams(vmem_limit_bytes=48 << 20),
        cost_estimate=pl.CostEstimate(
            flops=2 * rows * width * 896, bytes_accessed=8 << 20, transcendentals=0
        ),
        name="project",
    )(x, query_weight, fresh_weight)


def attend_kernel(parts_ref, cache_ref, out_ref, held_ref, sums_ref, result_ref, sems):
    copies = [
        pltpu.make_async_copy(cache_ref.at[t], held_ref.at[t], sems.at[t]) for t in range(4)
    ]
    for copy in copies:
        copy.start()
    total = parts_ref[0].astype(F32)
    for z in range(1, 4):
        total = total + parts_ref[z].astype(F32)
    total = total.astype(BF16).astype(F32).reshape(256, HEAD)
    for half in range(2):
        sums_ref[half] = total[:, half * 128 : half * 128 + 128]
        result_ref[half] = jnp.zeros((256, 128), F32)
    scale = HEAD ** (-0.5)
    for t in range(4):

        def slot(h):
            return jnp.concatenate(
                [sums_ref[half, pl.ds(h * 4 + t, 16, stride=16), :] for half in range(2)], axis=1
            )

        query = jnp.concatenate([slot(h) for h in range(3)], axis=0)
        columns = sums_ref[0, pl.ds(12 + t, 16, stride=16), :]
        fresh = [jnp.sum(columns[4 * b : 4 * b + 4], axis=0, keepdims=True) for b in range(4)]
        new_key = jnp.concatenate(fresh[:2], axis=1)
        new_value = jnp.concatenate(fresh[2:], axis=1)
        own = jnp.sum(query * new_key, axis=1, keepdims=True) * scale
        copies[t].wait()
        scores = (
            lax.dot_general(
                query.astype(BF16),
                held_ref[t, :, :HEAD],
                (((1,), (1,)), ((), ())),
                preferred_element_type=F32,
            )
            * scale
        )
        highest = jnp.maximum(jnp.max(scores, axis=1, keepdims=True), own)
        e_past = jnp.exp(scores - highest)
        e_own = jnp.exp(own - highest)
        total = jnp.sum(e_past, axis=1, keepdims=True) + e_own
        result = jnp.dot(e_past.astype(BF16), held_ref[t, :, HEAD:], preferred_element_type=F32)
        result = (result + e_own * new_value) / total
        for h in range(3):
            for half in range(2):
                result_ref[half, pl.ds(h * 4 + t, 16, stride=16), :] = result[
                    h * 16 : h * 16 + 16, half * 128 : half * 128 + 128
                ]
    whole = jnp.concatenate([result_ref[0], result_ref[1]], axis=1)
    whole = whole.reshape(16, 16, HEAD).astype(BF16)
    for z in range(4):
        out_ref[z] = whole


def attend(parts, cache):
    return pl.pallas_call(
        attend_kernel,
        in_specs=[
            pl.BlockSpec(memory_space=pltpu.VMEM),
            pl.BlockSpec(memory_space=pl.ANY),
        ],
        out_specs=pl.BlockSpec(memory_space=pltpu.VMEM),
        out_shape=jax.ShapeDtypeStruct((4, 16, 16, HEAD), BF16),
        scratch_shapes=[
            pltpu.VMEM(cache.shape, BF16),
            pltpu.VMEM((2, 256, 128), F32),
            pltpu.VMEM((2, 256, 128), F32),
            pltpu.SemaphoreType.DMA((4,)),
        ],
        compiler_params=pltpu.CompilerParams(vmem_limit_bytes=WIDE),
        cost_estimate=pl.CostEstimate(
            flops=4 * 4 * 48 * 2048 * 256, bytes_accessed=10 << 20, transcendentals=1 << 19
        ),
        name="attend",
    )(parts, cache)


def output_kernel(back_ref, other_ref, weight_ref, ffn_ref, out_ref, heads_ref):
    core = lax.axis_index("c")
    z_here = lax.axis_index("z")
    tile = out_ref.shape[1]

    @pl.when(pl.program_id(0) == 0)
    def _():
        low = lower_rows((8, 8, HEAD))
        for rel, ref in ((0, back_ref), (1, other_ref)):
            for z in range(4):
                even = ref[z, :, 0].astype(F32)
                odd = ref[z, :, 1].astype(F32)
                e0, e1, o0, o1 = even[:, :8], even[:, 8:], odd[:, :8], odd[:, 8:]
                heads = [
                    jnp.where(low, e0, pltpu.roll(o0, 4, 1)),
                    jnp.where(low, pltpu.roll(e0, 4, 1), o0),
                    jnp.where(low, e1, pltpu.roll(o1, 4, 1)),
                ]
                c = core if rel == 0 else 1 - core
                rows = pl.ds(pl.multiple_of(z * 128 + c * 64, 64), 64)
                for h in range(3):
                    heads_ref[rows, h * HEAD : (h + 1) * HEAD] = heads[h].reshape(64, HEAD).astype(BF16)

    terms = jnp.dot(heads_ref[...], weight_ref[...], preferred_element_type=F32)
    for z in range(4):
        away = (z_here - z + 4) % 4
        slot = jnp.where(away == 0, 0, jnp.where(away == 1, 1, jnp.where(away == 3, 2, 3)))
        for c in range(2):
            rel = jnp.where(core == c, 0, 4)
            here = pl.ds(pl.multiple_of((rel + slot) * 64, 64), 64)
            row = z * 128 + c * 64
            out_ref[row : row + 64, :] = (terms[row : row + 64] + ffn_ref[here, :]).astype(BF16)


def output(back, other, weight, ffn):
    rows, width = ffn.shape
    tile = 768
    whole = pl.BlockSpec((4, 8, 2, 16, HEAD), lambda i: (0, 0, 0, 0, 0), pipeline_mode=pl.Buffered(1))
    return pl.pallas_call(
        output_kernel,
        grid=(width // tile,),
        in_specs=[
            whole,
            whole,
            pl.BlockSpec((weight.shape[0], tile), lambda i: (0, i)),
            pl.BlockSpec((rows, tile), lambda i: (0, i)),
        ],
        out_specs=pl.BlockSpec((rows, tile), lambda i: (0, i)),
        out_shape=jax.ShapeDtypeStruct((rows, width), BF16),
        scratch_shapes=[pltpu.VMEM((rows, weight.shape[0]), BF16)],
        compiler_params=pltpu.CompilerParams(vmem_limit_bytes=20 << 20),
        cost_estimate=pl.CostEstimate(flops=2 * rows * width * 768, bytes_accessed=12 << 20, transcendentals=0),
        name="output",
    )(back, other, weight, ffn)


def add_kernel(pieces_ref, out_ref):
    total = pieces_ref[0].astype(F32)
    for i in range(1, pieces_ref.shape[0]):
        total = total + pieces_ref[i].astype(F32)
    out_ref[...] = total.astype(BF16)


def add_pieces(pieces):
    count, rows, width = pieces.shape
    tile = 768
    return pl.pallas_call(
        add_kernel,
        grid=(width // tile,),
        in_specs=[pl.BlockSpec((count, rows, tile), lambda i: (0, 0, i))],
        out_specs=pl.BlockSpec((rows, tile), lambda i: (0, i)),
        out_shape=jax.ShapeDtypeStruct((rows, width), BF16),
        compiler_params=pltpu.CompilerParams(vmem_limit_bytes=NARROW),
        name="add_pieces",
    )(pieces)


def body(residual, norm_gain, query_weight, kv_weight, cache, ffn_hidden, out_weight, down_weight):
    own_rows, width = residual.shape
    place = lax.axis_index(XY)
    rows = 16 * own_rows

    moments = row_moments(residual)
    moments = moments + lax.ppermute(moments, "c", SWAP)
    moments = moments + lax.ppermute(moments, "z", [(i, i ^ 1) for i in range(4)])
    more = lax.ppermute(moments, "z", [(i, i ^ 2) for i in range(4)])
    copies = normalize(residual, moments, more, norm_gain[None, :])
    copies, ffn_hidden, kv_weight = lax.optimization_barrier((copies, ffn_hidden, kv_weight))
    normed = lax.all_to_all(copies, XY, 0, 0).reshape(rows, width)

    hidden = jnp.concatenate(
        [ffn_hidden]
        + [lax.ppermute(ffn_hidden, "z", [(i, (i + k) % 4) for i in range(4)]) for k in (1, 3, 2)]
    )
    ffn = feed(hidden, lax.ppermute(hidden, "c", SWAP), down_weight)
    columns = kv_weight.shape[1]
    mask = jnp.arange(128)[None, :] // columns == place % 4
    fresh_weight = jnp.where(mask, jnp.tile(kv_weight, (1, 128 // columns)), 0)
    normed, fresh_weight, ffn = lax.optimization_barrier((normed, fresh_weight, ffn))

    mine, theirs = project(normed, query_weight, fresh_weight)
    paired = (mine.astype(F32) + lax.ppermute(theirs, "c", SWAP).astype(F32)).astype(BF16)
    parts = lax.all_to_all(paired.reshape(64, 16, HEAD), ZXY, 0, 0)

    attended = attend(parts.reshape(4, 16, 16, HEAD), cache)
    back = lax.all_to_all(attended.reshape(64, 16, HEAD), ZXY, 0, 0).reshape(4, 8, 2, 16, HEAD)
    other = lax.ppermute(back, "c", SWAP)
    terms = output(back, other, out_weight, ffn)
    pieces = lax.all_to_all(terms.reshape(16, own_rows, width), XY, 0, 0)
    return add_pieces(pieces)


def solution(mesh):
    fine = Mesh(mesh.devices.reshape(4, 2, 4, 4), ("z", "c", "x", "y"))
    placed = (
        P(XY, ZC),
        P(ZC),
        P(ZC, XY),
        P(ZC, XY),
        P(("z", "c", "x", "y"), None, None),
        P(ZC, XY),
        P(XY, ZC),
        P(XY, ZC),
    )
    return jax.shard_map(body, mesh=fine, in_specs=placed, out_specs=P(XY, ZC), check_vma=False)
```

```python
import functools

import jax
import jax.numpy as jnp
from jax import lax
from jax.experimental import pallas as pl
from jax.experimental.pallas import tpu as pltpu
from jax.sharding import Mesh, PartitionSpec as P

D = 18432
HEADS = 48
HEAD = 256
F32 = jnp.float32
BF16 = jnp.bfloat16
XY = ("x", "y")
ZC = ("z", "c")
ZXY = ("z", "x", "y")
SWAP = [(0, 1), (1, 0)]
WIDE = 58 << 20
NARROW = 8 << 20


def lower_rows(shape):
    return lax.broadcasted_iota(jnp.int32, shape, 1) < 4


def moments_kernel(residual_ref, out_ref, kept_ref):
    kept_ref[...] = residual_ref[...]
    values = residual_ref[...].astype(F32)
    sums = jnp.sum(values, axis=1, keepdims=True)
    squares = jnp.sum(values * values, axis=1, keepdims=True)
    lanes = lax.broadcasted_iota(jnp.int32, out_ref.shape, 1)
    out_ref[...] = jnp.where(lanes < 64, sums, squares)


def row_moments(residual):
    return pl.pallas_call(
        moments_kernel,
        out_shape=[
            jax.ShapeDtypeStruct((residual.shape[0], 128), F32),
            jax.ShapeDtypeStruct(residual.shape, BF16),
        ],
        compiler_params=pltpu.CompilerParams(vmem_limit_bytes=NARROW),
        name="row_moments",
    )(residual)


def normalize_kernel(residual_ref, moments_ref, more_ref, gain_ref, out_ref):
    moments = moments_ref[...] + more_ref[...]
    mean = moments[:, 0:1] / D
    var = moments[:, 64:65] / D - mean * mean
    values = residual_ref[...].astype(F32)
    normed = ((values - mean) * lax.rsqrt(var + 1e-05) * gain_ref[...]).astype(BF16)
    for i in range(out_ref.shape[0]):
        out_ref[i] = normed


def normalize(residual, moments, more, gain):
    rows, width = residual.shape
    return pl.pallas_call(
        normalize_kernel,
        out_shape=jax.ShapeDtypeStruct((16, rows, width), BF16),
        compiler_params=pltpu.CompilerParams(vmem_limit_bytes=NARROW),
        cost_estimate=pl.CostEstimate(flops=1 << 20, bytes_accessed=24 << 20, transcendentals=0),
        name="normalize",
    )(residual, moments, more, gain)


def feed_kernel(*refs):
    hidden_refs, (weight_ref, out_ref, x_ref) = refs[:8], refs[8:]

    @pl.when(pl.program_id(0) + lax.axis_index("c") * 4 % 4 == 0)
    def _():
        for i, ref in enumerate(hidden_refs):
            x_ref[i * 64 : i * 64 + 64, :] = ref[...]

    out_ref[...] = jnp.dot(x_ref[...], weight_ref[...], preferred_element_type=F32)


def feed(hidden, weight):
    rows, depth = 64 * len(hidden), hidden[0].shape[1]
    width = weight.shape[1]
    tile = 768
    whole = pl.BlockSpec((64, depth), lambda i: (0, 0), pipeline_mode=pl.Buffered(1))
    return pl.pallas_call(
        feed_kernel,
        grid=(width // tile,),
        in_specs=[whole] * len(hidden) + [pl.BlockSpec((depth, tile), lambda i: (0, i))],
        out_specs=pl.BlockSpec((rows, tile), lambda i: (0, i)),
        out_shape=jax.ShapeDtypeStruct((rows, width), F32),
        scratch_shapes=[pltpu.VMEM((rows, depth), BF16)],
        compiler_params=pltpu.CompilerParams(vmem_limit_bytes=20 << 20),
        cost_estimate=pl.CostEstimate(flops=1 << 31, bytes_accessed=1, transcendentals=0),
        name="feed",
    )(*hidden, weight)


def project_kernel(x_ref, query_ref, fresh_ref, mine_ref, theirs_ref, slots_ref):
    core = lax.axis_index("c")
    step = pl.program_id(0)

    @pl.when(step < 3)
    def _():
        slots_ref[step] = jnp.dot(x_ref[...], query_ref[...], preferred_element_type=F32)

    @pl.when(step == 3)
    def _():
        fresh = jnp.dot(x_ref[...], fresh_ref[...], preferred_element_type=F32)
        fresh = jnp.concatenate([fresh, jnp.zeros_like(fresh)], axis=1)
        low = lower_rows((8, 8, HEAD))
        for block in range(8):
            z, c = block // 2, block % 2
            rows = slice(block * 64, block * 64 + 64)
            s = [slots_ref[h, rows, :] for h in range(3)] + [fresh[rows]]
            s = [v.reshape(8, 8, HEAD) for v in s]
            r = [pltpu.roll(v, 4, 1) for v in s]
            even = jnp.concatenate([jnp.where(low, s[0], r[1]), jnp.where(low, s[2], r[3])], axis=1)
            odd = jnp.concatenate([jnp.where(low, r[0], s[1]), jnp.where(low, r[2], s[3])], axis=1)

            def put(ref, z=z, even=even, odd=odd):
                ref[z, :, 0] = even.astype(BF16)
                ref[z, :, 1] = odd.astype(BF16)

            pl.when(core == c)(functools.partial(put, mine_ref))
            pl.when(core != c)(functools.partial(put, theirs_ref))


def project(x, query_weight, fresh_weight):
    rows, width = x.shape
    out = jax.ShapeDtypeStruct((4, 8, 2, 16, HEAD), BF16)
    return pl.pallas_call(
        project_kernel,
        grid=(4,),
        in_specs=[
            pl.BlockSpec((rows, width), lambda i: (0, 0), pipeline_mode=pl.Buffered(1)),
            pl.BlockSpec((width, HEAD), lambda i: (0, jnp.minimum(i, 2))),
            pl.BlockSpec(fresh_weight.shape, lambda i: (0, 0), pipeline_mode=pl.Buffered(1)),
        ],
        out_specs=[pl.BlockSpec(out.shape, lambda i: (0, 0, 0, 0, 0))] * 2,
        out_shape=[out, out],
        scratch_shapes=[pltpu.VMEM((3, rows, HEAD), F32)],
        compiler_params=pltpu.CompilerParams(vmem_limit_bytes=24 << 20),
        cost_estimate=pl.CostEstimate(
            flops=2 * rows * width * 896, bytes_accessed=8 << 20, transcendentals=0
        ),
        name="project",
    )(x, query_weight, fresh_weight)


def attend_kernel(parts_ref, cache_ref, out_ref, sums_ref, result_ref):
    t = pl.program_id(0)

    @pl.when(t == 0)
    def _():
        total = parts_ref[0].astype(F32)
        for z in range(1, 4):
            total = total + parts_ref[z].astype(F32)
        total = total.astype(BF16).astype(F32).reshape(256, HEAD)
        for half in range(2):
            sums_ref[half] = total[:, half * 128 : half * 128 + 128]
            result_ref[half] = jnp.zeros((256, 128), F32)

    def slot(h):
        return jnp.concatenate(
            [sums_ref[half, pl.ds(h * 4 + t, 16, stride=16), :] for half in range(2)], axis=1
        )

    query = jnp.concatenate([slot(h) for h in range(3)], axis=0)
    columns = sums_ref[0, pl.ds(12 + t, 16, stride=16), :]
    fresh = [jnp.sum(columns[4 * b : 4 * b + 4], axis=0, keepdims=True) for b in range(4)]
    new_key = jnp.concatenate(fresh[:2], axis=1)
    new_value = jnp.concatenate(fresh[2:], axis=1)
    scale = HEAD ** (-0.5)
    own = jnp.sum(query * new_key, axis=1, keepdims=True) * scale
    scores = (
        lax.dot_general(
            query.astype(BF16),
            cache_ref[0, :, :HEAD],
            (((1,), (1,)), ((), ())),
            preferred_element_type=F32,
        )
        * scale
    )
    highest = jnp.maximum(jnp.max(scores, axis=1, keepdims=True), own)
    e_past = jnp.exp(scores - highest)
    e_own = jnp.exp(own - highest)
    total = jnp.sum(e_past, axis=1, keepdims=True) + e_own
    result = jnp.dot(e_past.astype(BF16), cache_ref[0, :, HEAD:], preferred_element_type=F32)
    result = (result + e_own * new_value) / total
    for h in range(3):
        for half in range(2):
            result_ref[half, pl.ds(h * 4 + t, 16, stride=16), :] = result[
                h * 16 : h * 16 + 16, half * 128 : half * 128 + 128
            ]

    @pl.when(t + lax.axis_index("c") * 4 % 4 == 3)
    def _():
        whole = jnp.concatenate([result_ref[0], result_ref[1]], axis=1)
        whole = whole.reshape(16, 16, HEAD).astype(BF16)
        for z in range(4):
            out_ref[z] = whole


def attend(parts, cache):
    return pl.pallas_call(
        attend_kernel,
        grid=(4,),
        in_specs=[
            pl.BlockSpec((4, 16, 16, HEAD), lambda t: (0, 0, 0, 0)),
            pl.BlockSpec((1,) + cache.shape[1:], lambda t: (t, 0, 0)),
        ],
        out_specs=pl.BlockSpec((4, 16, 16, HEAD), lambda t: (0, 0, 0, 0)),
        out_shape=jax.ShapeDtypeStruct((4, 16, 16, HEAD), BF16),
        scratch_shapes=[pltpu.VMEM((2, 256, 128), F32), pltpu.VMEM((2, 256, 128), F32)],
        compiler_params=pltpu.CompilerParams(vmem_limit_bytes=12 << 20),
        cost_estimate=pl.CostEstimate(
            flops=4 * 4 * 48 * 2048 * 256, bytes_accessed=10 << 20, transcendentals=1 << 19
        ),
        name="attend",
    )(parts, cache)


def output_kernel(back_ref, other_ref, weight_ref, ffn_ref, out_ref, heads_ref):
    core = lax.axis_index("c")
    z_here = lax.axis_index("z")
    tile = out_ref.shape[1]

    @pl.when(pl.program_id(0) == 0)
    def _():
        low = lower_rows((8, 8, HEAD))
        for rel, ref in ((0, back_ref), (1, other_ref)):
            for z in range(4):
                even = ref[z, :, 0].astype(F32)
                odd = ref[z, :, 1].astype(F32)
                e0, e1, o0, o1 = even[:, :8], even[:, 8:], odd[:, :8], odd[:, 8:]
                heads = [
                    jnp.where(low, e0, pltpu.roll(o0, 4, 1)),
                    jnp.where(low, pltpu.roll(e0, 4, 1), o0),
                    jnp.where(low, e1, pltpu.roll(o1, 4, 1)),
                ]
                c = core if rel == 0 else 1 - core
                rows = pl.ds(pl.multiple_of(z * 128 + c * 64, 64), 64)
                for h in range(3):
                    heads_ref[rows, h * HEAD : (h + 1) * HEAD] = heads[h].reshape(64, HEAD).astype(BF16)

    terms = jnp.dot(heads_ref[...], weight_ref[...], preferred_element_type=F32)
    for z in range(4):
        away = (z_here - z + 4) % 4
        slot = jnp.where(away == 0, 0, jnp.where(away == 1, 1, jnp.where(away == 3, 2, 3)))
        for c in range(2):
            rel = jnp.where(core == c, 0, 4)
            here = pl.ds(pl.multiple_of((rel + slot) * 64, 64), 64)
            row = z * 128 + c * 64
            out_ref[row : row + 64, :] = (terms[row : row + 64] + ffn_ref[here, :]).astype(BF16)


def output(back, other, weight, ffn):
    rows, width = ffn.shape
    tile = 768
    whole = pl.BlockSpec((4, 8, 2, 16, HEAD), lambda i: (0, 0, 0, 0, 0), pipeline_mode=pl.Buffered(1))
    return pl.pallas_call(
        output_kernel,
        grid=(width // tile,),
        in_specs=[
            whole,
            whole,
            pl.BlockSpec((weight.shape[0], tile), lambda i: (0, i)),
            pl.BlockSpec((rows, tile), lambda i: (0, i)),
        ],
        out_specs=pl.BlockSpec((rows, tile), lambda i: (0, i)),
        out_shape=jax.ShapeDtypeStruct((rows, width), BF16),
        scratch_shapes=[pltpu.VMEM((rows, weight.shape[0]), BF16)],
        compiler_params=pltpu.CompilerParams(vmem_limit_bytes=20 << 20),
        cost_estimate=pl.CostEstimate(flops=2 * rows * width * 768, bytes_accessed=12 << 20, transcendentals=0),
        name="output",
    )(back, other, weight, ffn)


def add_kernel(pieces_ref, out_ref):
    total = pieces_ref[0].astype(F32)
    for i in range(1, pieces_ref.shape[0]):
        total = total + pieces_ref[i].astype(F32)
    out_ref[...] = total.astype(BF16)


def add_pieces(pieces):
    count, rows, width = pieces.shape
    tile = 768
    return pl.pallas_call(
        add_kernel,
        grid=(width // tile,),
        in_specs=[pl.BlockSpec((count, rows, tile), lambda i: (0, 0, i))],
        out_specs=pl.BlockSpec((rows, tile), lambda i: (0, i)),
        out_shape=jax.ShapeDtypeStruct((rows, width), BF16),
        compiler_params=pltpu.CompilerParams(vmem_limit_bytes=NARROW),
        name="add_pieces",
    )(pieces)


def body(residual, norm_gain, query_weight, kv_weight, cache, ffn_hidden, out_weight, down_weight):
    own_rows, width = residual.shape
    place = lax.axis_index(XY)
    rows = 16 * own_rows

    moments, kept = row_moments(residual)
    moments = moments + lax.ppermute(moments, "c", SWAP)
    moments = moments + lax.ppermute(moments, "z", [(i, i ^ 1) for i in range(4)])
    more = lax.ppermute(moments, "z", [(i, i ^ 2) for i in range(4)])
    copies = normalize(kept, moments, more, norm_gain[None, :])
    copies, ffn_hidden, kv_weight = lax.optimization_barrier((copies, ffn_hidden, kv_weight))
    normed = lax.all_to_all(copies, XY, 0, 0).reshape(rows, width)

    hidden = [ffn_hidden] + [
        lax.ppermute(ffn_hidden, "z", [(i, (i + k) % 4) for i in range(4)]) for k in (1, 3, 2)
    ]
    ffn = feed(hidden + [lax.ppermute(v, "c", SWAP) for v in hidden], down_weight)
    columns = kv_weight.shape[1]
    mask = jnp.arange(128)[None, :] // columns == place % 4
    fresh_weight = jnp.where(mask, jnp.tile(kv_weight, (1, 128 // columns)), 0)
    normed, fresh_weight, ffn = lax.optimization_barrier((normed, fresh_weight, ffn))

    mine, theirs = project(normed, query_weight, fresh_weight)
    paired = (mine.astype(F32) + lax.ppermute(theirs, "c", SWAP).astype(F32)).astype(BF16)
    parts = lax.all_to_all(paired.reshape(64, 16, HEAD), ZXY, 0, 0)

    attended = attend(parts.reshape(4, 16, 16, HEAD), cache)
    back = lax.all_to_all(attended.reshape(64, 16, HEAD), ZXY, 0, 0).reshape(4, 8, 2, 16, HEAD)
    other = lax.ppermute(back, "c", SWAP)
    terms = output(back, other, out_weight, ffn)
    pieces = lax.all_to_all(terms.reshape(16, own_rows, width), XY, 0, 0)
    return add_pieces(pieces)


def solution(mesh):
    fine = Mesh(mesh.devices.reshape(4, 2, 4, 4), ("z", "c", "x", "y"))
    placed = (
        P(XY, ZC),
        P(ZC),
        P(ZC, XY),
        P(ZC, XY),
        P(("z", "c", "x", "y"), None, None),
        P(ZC, XY),
        P(XY, ZC),
        P(XY, ZC),
    )
    return jax.shard_map(body, mesh=fine, in_specs=placed, out_specs=P(XY, ZC), check_vma=False)
```

```python
import functools

import jax
import jax.numpy as jnp
from jax import lax
from jax.experimental import pallas as pl
from jax.experimental.pallas import tpu as pltpu
from jax.sharding import Mesh, PartitionSpec as P

D = 18432
HEADS = 48
HEAD = 256
F32 = jnp.float32
BF16 = jnp.bfloat16
XY = ("x", "y")
ZC = ("z", "c")
ZXY = ("z", "x", "y")
SWAP = [(0, 1), (1, 0)]
WIDE = 58 << 20
NARROW = 8 << 20


def lower_rows(shape):
    return lax.broadcasted_iota(jnp.int32, shape, 1) < 4


def moments_kernel(residual_ref, out_ref, kept_ref):
    kept_ref[...] = residual_ref[...]
    values = residual_ref[...].astype(F32)
    sums = jnp.sum(values, axis=1, keepdims=True)
    squares = jnp.sum(values * values, axis=1, keepdims=True)
    lanes = lax.broadcasted_iota(jnp.int32, out_ref.shape, 1)
    out_ref[...] = jnp.where(lanes < 64, sums, squares)


def row_moments(residual):
    return pl.pallas_call(
        moments_kernel,
        out_shape=[
            jax.ShapeDtypeStruct((residual.shape[0], 128), F32),
            jax.ShapeDtypeStruct(residual.shape, BF16),
        ],
        compiler_params=pltpu.CompilerParams(vmem_limit_bytes=NARROW),
        name="row_moments",
    )(residual)


def normalize_kernel(residual_ref, *refs):
    moments_refs, (gain_ref, out_ref) = refs[:4], refs[4:]
    moments = moments_refs[0][...]
    for ref in moments_refs[1:]:
        moments = moments + ref[...]
    mean = moments[:, 0:1] / D
    var = moments[:, 64:65] / D - mean * mean
    values = residual_ref[...].astype(F32)
    normed = ((values - mean) * lax.rsqrt(var + 1e-05) * gain_ref[...]).astype(BF16)
    for i in range(out_ref.shape[0]):
        out_ref[i] = normed


def normalize(residual, moments, gain):
    rows, width = residual.shape
    return pl.pallas_call(
        normalize_kernel,
        out_shape=jax.ShapeDtypeStruct((16, rows, width), BF16),
        compiler_params=pltpu.CompilerParams(vmem_limit_bytes=NARROW),
        cost_estimate=pl.CostEstimate(flops=1 << 20, bytes_accessed=24 << 20, transcendentals=0),
        name="normalize",
    )(residual, *moments, gain)


def feed_kernel(*refs):
    hidden_refs, (weight_ref, out_ref, x_ref) = refs[:8], refs[8:]

    @pl.when(pl.program_id(0) + lax.axis_index("c") * 4 % 4 == 0)
    def _():
        for i, ref in enumerate(hidden_refs):
            x_ref[i * 64 : i * 64 + 64, :] = ref[...]

    out_ref[...] = jnp.dot(x_ref[...], weight_ref[...], preferred_element_type=F32)


def feed(hidden, weight):
    rows, depth = 64 * len(hidden), hidden[0].shape[1]
    width = weight.shape[1]
    tile = 768
    whole = pl.BlockSpec((64, depth), lambda i: (0, 0), pipeline_mode=pl.Buffered(1))
    return pl.pallas_call(
        feed_kernel,
        grid=(width // tile,),
        in_specs=[whole] * len(hidden) + [pl.BlockSpec((depth, tile), lambda i: (0, i))],
        out_specs=pl.BlockSpec((rows, tile), lambda i: (0, i)),
        out_shape=jax.ShapeDtypeStruct((rows, width), F32),
        scratch_shapes=[pltpu.VMEM((rows, depth), BF16)],
        compiler_params=pltpu.CompilerParams(vmem_limit_bytes=20 << 20),
        cost_estimate=pl.CostEstimate(flops=1 << 31, bytes_accessed=1, transcendentals=0),
        name="feed",
    )(*hidden, weight)


def project_kernel(x_ref, query_ref, fresh_ref, mine_ref, theirs_ref, slots_ref):
    core = lax.axis_index("c")
    step = pl.program_id(0)

    @pl.when(step < 3)
    def _():
        slots_ref[step] = jnp.dot(x_ref[...], query_ref[...], preferred_element_type=F32)

    @pl.when(step == 3)
    def _():
        fresh = jnp.dot(x_ref[...], fresh_ref[...], preferred_element_type=F32)
        fresh = jnp.concatenate([fresh, jnp.zeros_like(fresh)], axis=1)
        low = lower_rows((8, 8, HEAD))
        for block in range(8):
            z, c = block // 2, block % 2
            rows = slice(block * 64, block * 64 + 64)
            s = [slots_ref[h, rows, :] for h in range(3)] + [fresh[rows]]
            s = [v.reshape(8, 8, HEAD) for v in s]
            r = [pltpu.roll(v, 4, 1) for v in s]
            even = jnp.concatenate([jnp.where(low, s[0], r[1]), jnp.where(low, s[2], r[3])], axis=1)
            odd = jnp.concatenate([jnp.where(low, r[0], s[1]), jnp.where(low, r[2], s[3])], axis=1)

            def put(ref, z=z, even=even, odd=odd):
                ref[z, :, 0] = even.astype(BF16)
                ref[z, :, 1] = odd.astype(BF16)

            pl.when(core == c)(functools.partial(put, mine_ref))
            pl.when(core != c)(functools.partial(put, theirs_ref))


def project(x, query_weight, fresh_weight):
    rows, width = x.shape
    out = jax.ShapeDtypeStruct((4, 8, 2, 16, HEAD), BF16)
    return pl.pallas_call(
        project_kernel,
        grid=(4,),
        in_specs=[
            pl.BlockSpec((rows, width), lambda i: (0, 0), pipeline_mode=pl.Buffered(1)),
            pl.BlockSpec((width, HEAD), lambda i: (0, jnp.minimum(i, 2))),
            pl.BlockSpec(fresh_weight.shape, lambda i: (0, 0), pipeline_mode=pl.Buffered(1)),
        ],
        out_specs=[pl.BlockSpec(out.shape, lambda i: (0, 0, 0, 0, 0))] * 2,
        out_shape=[out, out],
        scratch_shapes=[pltpu.VMEM((3, rows, HEAD), F32)],
        compiler_params=pltpu.CompilerParams(vmem_limit_bytes=24 << 20),
        cost_estimate=pl.CostEstimate(
            flops=2 * rows * width * 896, bytes_accessed=8 << 20, transcendentals=0
        ),
        name="project",
    )(x, query_weight, fresh_weight)


def attend_kernel(parts_ref, cache_ref, out_ref, sums_ref, result_ref):
    t = pl.program_id(0)

    @pl.when(t == 0)
    def _():
        total = parts_ref[0].astype(F32)
        for z in range(1, 4):
            total = total + parts_ref[z].astype(F32)
        total = total.astype(BF16).astype(F32).reshape(256, HEAD)
        for half in range(2):
            sums_ref[half] = total[:, half * 128 : half * 128 + 128]
            result_ref[half] = jnp.zeros((256, 128), F32)

    def slot(h):
        return jnp.concatenate(
            [sums_ref[half, pl.ds(h * 4 + t, 16, stride=16), :] for half in range(2)], axis=1
        )

    query = jnp.concatenate([slot(h) for h in range(3)], axis=0)
    columns = sums_ref[0, pl.ds(12 + t, 16, stride=16), :]
    fresh = [jnp.sum(columns[4 * b : 4 * b + 4], axis=0, keepdims=True) for b in range(4)]
    new_key = jnp.concatenate(fresh[:2], axis=1)
    new_value = jnp.concatenate(fresh[2:], axis=1)
    scale = HEAD ** (-0.5)
    own = jnp.sum(query * new_key, axis=1, keepdims=True) * scale
    scores = (
        lax.dot_general(
            query.astype(BF16),
            cache_ref[0, :, :HEAD],
            (((1,), (1,)), ((), ())),
            preferred_element_type=F32,
        )
        * scale
    )
    highest = jnp.maximum(jnp.max(scores, axis=1, keepdims=True), own)
    e_past = jnp.exp(scores - highest)
    e_own = jnp.exp(own - highest)
    total = jnp.sum(e_past, axis=1, keepdims=True) + e_own
    result = jnp.dot(e_past.astype(BF16), cache_ref[0, :, HEAD:], preferred_element_type=F32)
    result = (result + e_own * new_value) / total
    for h in range(3):
        for half in range(2):
            result_ref[half, pl.ds(h * 4 + t, 16, stride=16), :] = result[
                h * 16 : h * 16 + 16, half * 128 : half * 128 + 128
            ]

    @pl.when(t + lax.axis_index("c") * 4 % 4 == 3)
    def _():
        whole = jnp.concatenate([result_ref[0], result_ref[1]], axis=1)
        whole = whole.reshape(16, 16, HEAD).astype(BF16)
        for z in range(4):
            out_ref[z] = whole


def attend(parts, cache):
    return pl.pallas_call(
        attend_kernel,
        grid=(4,),
        in_specs=[
            pl.BlockSpec((4, 16, 16, HEAD), lambda t: (0, 0, 0, 0)),
            pl.BlockSpec((1,) + cache.shape[1:], lambda t: (t, 0, 0)),
        ],
        out_specs=pl.BlockSpec((4, 16, 16, HEAD), lambda t: (0, 0, 0, 0)),
        out_shape=jax.ShapeDtypeStruct((4, 16, 16, HEAD), BF16),
        scratch_shapes=[pltpu.VMEM((2, 256, 128), F32), pltpu.VMEM((2, 256, 128), F32)],
        compiler_params=pltpu.CompilerParams(vmem_limit_bytes=12 << 20),
        cost_estimate=pl.CostEstimate(
            flops=4 * 4 * 48 * 2048 * 256, bytes_accessed=10 << 20, transcendentals=1 << 19
        ),
        name="attend",
    )(parts, cache)


def output_kernel(back_ref, other_ref, weight_ref, ffn_ref, out_ref, heads_ref):
    core = lax.axis_index("c")
    z_here = lax.axis_index("z")
    tile = out_ref.shape[1]

    @pl.when(pl.program_id(0) == 0)
    def _():
        low = lower_rows((8, 8, HEAD))
        for rel, ref in ((0, back_ref), (1, other_ref)):
            for z in range(4):
                even = ref[z, :, 0].astype(F32)
                odd = ref[z, :, 1].astype(F32)
                e0, e1, o0, o1 = even[:, :8], even[:, 8:], odd[:, :8], odd[:, 8:]
                heads = [
                    jnp.where(low, e0, pltpu.roll(o0, 4, 1)),
                    jnp.where(low, pltpu.roll(e0, 4, 1), o0),
                    jnp.where(low, e1, pltpu.roll(o1, 4, 1)),
                ]
                c = core if rel == 0 else 1 - core
                rows = pl.ds(pl.multiple_of(z * 128 + c * 64, 64), 64)
                for h in range(3):
                    heads_ref[rows, h * HEAD : (h + 1) * HEAD] = heads[h].reshape(64, HEAD).astype(BF16)

    terms = jnp.dot(heads_ref[...], weight_ref[...], preferred_element_type=F32)
    for z in range(4):
        away = (z_here - z + 4) % 4
        slot = jnp.where(away == 0, 0, jnp.where(away == 1, 1, jnp.where(away == 3, 2, 3)))
        for c in range(2):
            rel = jnp.where(core == c, 0, 4)
            here = pl.ds(pl.multiple_of((rel + slot) * 64, 64), 64)
            row = z * 128 + c * 64
            out_ref[row : row + 64, :] = (terms[row : row + 64] + ffn_ref[here, :]).astype(BF16)


def output(back, other, weight, ffn):
    rows, width = ffn.shape
    tile = 768
    whole = pl.BlockSpec((4, 8, 2, 16, HEAD), lambda i: (0, 0, 0, 0, 0), pipeline_mode=pl.Buffered(1))
    return pl.pallas_call(
        output_kernel,
        grid=(width // tile,),
        in_specs=[
            whole,
            whole,
            pl.BlockSpec((weight.shape[0], tile), lambda i: (0, i)),
            pl.BlockSpec((rows, tile), lambda i: (0, i)),
        ],
        out_specs=pl.BlockSpec((rows, tile), lambda i: (0, i)),
        out_shape=jax.ShapeDtypeStruct((rows, width), BF16),
        scratch_shapes=[pltpu.VMEM((rows, weight.shape[0]), BF16)],
        compiler_params=pltpu.CompilerParams(vmem_limit_bytes=20 << 20),
        cost_estimate=pl.CostEstimate(flops=2 * rows * width * 768, bytes_accessed=12 << 20, transcendentals=0),
        name="output",
    )(back, other, weight, ffn)


def add_kernel(pieces_ref, out_ref):
    @pl.loop(0, out_ref.shape[1] // 256)
    def _(n):
        columns = pl.ds(pl.multiple_of(n * 256, 256), 256)
        total = pieces_ref[0, :, columns].astype(F32)
        for i in range(1, pieces_ref.shape[0]):
            total = total + pieces_ref[i, :, columns].astype(F32)
        out_ref[:, columns] = total.astype(BF16)


def add_pieces(pieces):
    return pl.pallas_call(
        add_kernel,
        in_specs=[pl.BlockSpec(memory_space=pltpu.VMEM)],
        out_specs=pl.BlockSpec(memory_space=pltpu.VMEM),
        out_shape=jax.ShapeDtypeStruct(pieces.shape[1:], BF16),
        compiler_params=pltpu.CompilerParams(vmem_limit_bytes=NARROW),
        name="add_pieces",
    )(pieces)


def body(residual, norm_gain, query_weight, kv_weight, cache, ffn_hidden, out_weight, down_weight):
    own_rows, width = residual.shape
    place = lax.axis_index(XY)
    rows = 16 * own_rows

    moments, kept = row_moments(residual)
    moments = moments + lax.ppermute(moments, "c", SWAP)
    moments = [moments] + [
        lax.ppermute(moments, "z", [(i, (i + k) % 4) for i in range(4)]) for k in (2, 1, 3)
    ]
    copies = normalize(kept, moments, norm_gain[None, :])
    copies, ffn_hidden, kv_weight = lax.optimization_barrier((copies, ffn_hidden, kv_weight))
    normed = lax.all_to_all(copies, XY, 0, 0).reshape(rows, width)

    hidden = [ffn_hidden] + [
        lax.ppermute(ffn_hidden, "z", [(i, (i + k) % 4) for i in range(4)]) for k in (1, 3, 2)
    ]
    ffn = feed(hidden + [lax.ppermute(v, "c", SWAP) for v in hidden], down_weight)
    columns = kv_weight.shape[1]
    mask = jnp.arange(128)[None, :] // columns == place % 4
    fresh_weight = jnp.where(mask, jnp.tile(kv_weight, (1, 128 // columns)), 0)
    normed, fresh_weight, ffn = lax.optimization_barrier((normed, fresh_weight, ffn))

    mine, theirs = project(normed, query_weight, fresh_weight)
    paired = (mine.astype(F32) + lax.ppermute(theirs, "c", SWAP).astype(F32)).astype(BF16)
    parts = lax.all_to_all(paired.reshape(64, 16, HEAD), ZXY, 0, 0)

    attended = attend(parts.reshape(4, 16, 16, HEAD), cache)
    back = lax.all_to_all(attended.reshape(64, 16, HEAD), ZXY, 0, 0).reshape(4, 8, 2, 16, HEAD)
    other = lax.ppermute(back, "c", SWAP)
    terms = output(back, other, out_weight, ffn)
    pieces = lax.all_to_all(terms.reshape(16, own_rows, width), XY, 0, 0)
    return add_pieces(pieces)


def solution(mesh):
    fine = Mesh(mesh.devices.reshape(4, 2, 4, 4), ("z", "c", "x", "y"))
    placed = (
        P(XY, ZC),
        P(ZC),
        P(ZC, XY),
        P(ZC, XY),
        P(("z", "c", "x", "y"), None, None),
        P(ZC, XY),
        P(XY, ZC),
        P(XY, ZC),
    )
    return jax.shard_map(body, mesh=fine, in_specs=placed, out_specs=P(XY, ZC), check_vma=False)
```

```python
import functools

import jax
import jax.numpy as jnp
from jax import lax
from jax.experimental import pallas as pl
from jax.experimental.pallas import tpu as pltpu
from jax.sharding import Mesh, PartitionSpec as P

D = 18432
HEADS = 48
HEAD = 256
F32 = jnp.float32
BF16 = jnp.bfloat16
XY = ("x", "y")
ZC = ("z", "c")
ZXY = ("z", "x", "y")
SWAP = [(0, 1), (1, 0)]
WIDE = 58 << 20
NARROW = 8 << 20


def lower_rows(shape):
    return lax.broadcasted_iota(jnp.int32, shape, 1) < 4


def moments_kernel(residual_ref, out_ref, kept_ref):
    kept_ref[...] = residual_ref[...]
    values = residual_ref[...].astype(F32)
    sums = jnp.sum(values, axis=1, keepdims=True)
    squares = jnp.sum(values * values, axis=1, keepdims=True)
    lanes = lax.broadcasted_iota(jnp.int32, out_ref.shape, 1)
    out_ref[...] = jnp.where(lanes < 64, sums, squares)


def row_moments(residual):
    return pl.pallas_call(
        moments_kernel,
        out_shape=[
            jax.ShapeDtypeStruct((residual.shape[0], 128), F32),
            jax.ShapeDtypeStruct(residual.shape, BF16),
        ],
        compiler_params=pltpu.CompilerParams(vmem_limit_bytes=NARROW),
        name="row_moments",
    )(residual)


def normalize_kernel(residual_ref, *refs):
    moments_refs, (gain_ref, out_ref) = refs[:4], refs[4:]
    moments = moments_refs[0][...]
    for ref in moments_refs[1:]:
        moments = moments + ref[...]
    mean = moments[:, 0:1] / D
    var = moments[:, 64:65] / D - mean * mean
    values = residual_ref[...].astype(F32)
    normed = ((values - mean) * lax.rsqrt(var + 1e-05) * gain_ref[...]).astype(BF16)
    for i in range(out_ref.shape[0]):
        out_ref[i] = normed


def normalize(residual, moments, gain):
    rows, width = residual.shape
    return pl.pallas_call(
        normalize_kernel,
        out_shape=jax.ShapeDtypeStruct((16, rows, width), BF16),
        compiler_params=pltpu.CompilerParams(vmem_limit_bytes=NARROW),
        cost_estimate=pl.CostEstimate(flops=1 << 20, bytes_accessed=24 << 20, transcendentals=0),
        name="normalize",
    )(residual, *moments, gain)


def feed_kernel(*refs):
    hidden_refs, (weight_ref, out_ref, x_ref) = refs[:8], refs[8:]

    @pl.when(pl.program_id(0) + lax.axis_index("c") * 4 % 4 == 0)
    def _():
        for i, ref in enumerate(hidden_refs):
            x_ref[i * 64 : i * 64 + 64, :] = ref[...]

    out_ref[...] = jnp.dot(x_ref[...], weight_ref[...], preferred_element_type=F32)


def feed(hidden, weight):
    rows, depth = 64 * len(hidden), hidden[0].shape[1]
    width = weight.shape[1]
    tile = 1152
    whole = pl.BlockSpec((64, depth), lambda i: (0, 0), pipeline_mode=pl.Buffered(1))
    return pl.pallas_call(
        feed_kernel,
        grid=(width // tile,),
        in_specs=[whole] * len(hidden) + [pl.BlockSpec((depth, tile), lambda i: (0, i))],
        out_specs=pl.BlockSpec((rows, tile), lambda i: (0, i)),
        out_shape=jax.ShapeDtypeStruct((rows, width), F32),
        scratch_shapes=[pltpu.VMEM((rows, depth), BF16)],
        compiler_params=pltpu.CompilerParams(vmem_limit_bytes=28 << 20),
        cost_estimate=pl.CostEstimate(flops=1 << 31, bytes_accessed=1, transcendentals=0),
        name="feed",
    )(*hidden, weight)


def project_kernel(x_ref, query_ref, fresh_ref, mine_ref, theirs_ref, slots_ref):
    core = lax.axis_index("c")
    step = pl.program_id(0)

    @pl.when(step < 3)
    def _():
        slots_ref[step] = jnp.dot(x_ref[...], query_ref[...], preferred_element_type=F32)

    @pl.when(step == 3)
    def _():
        fresh = jnp.dot(x_ref[...], fresh_ref[...], preferred_element_type=F32)
        fresh = jnp.concatenate([fresh, jnp.zeros_like(fresh)], axis=1)
        low = lower_rows((8, 8, HEAD))
        for block in range(8):
            z, c = block // 2, block % 2
            rows = slice(block * 64, block * 64 + 64)
            s = [slots_ref[h, rows, :] for h in range(3)] + [fresh[rows]]
            s = [v.reshape(8, 8, HEAD) for v in s]
            r = [pltpu.roll(v, 4, 1) for v in s]
            even = jnp.concatenate([jnp.where(low, s[0], r[1]), jnp.where(low, s[2], r[3])], axis=1)
            odd = jnp.concatenate([jnp.where(low, r[0], s[1]), jnp.where(low, r[2], s[3])], axis=1)

            def put(ref, z=z, even=even, odd=odd):
                ref[z, :, 0] = even.astype(BF16)
                ref[z, :, 1] = odd.astype(BF16)

            pl.when(core == c)(functools.partial(put, mine_ref))
            pl.when(core != c)(functools.partial(put, theirs_ref))


def project(x, query_weight, fresh_weight):
    rows, width = x.shape
    out = jax.ShapeDtypeStruct((4, 8, 2, 16, HEAD), BF16)
    return pl.pallas_call(
        project_kernel,
        grid=(4,),
        in_specs=[
            pl.BlockSpec((rows, width), lambda i: (0, 0), pipeline_mode=pl.Buffered(1)),
            pl.BlockSpec((width, HEAD), lambda i: (0, jnp.minimum(i, 2))),
            pl.BlockSpec(fresh_weight.shape, lambda i: (0, 0), pipeline_mode=pl.Buffered(1)),
        ],
        out_specs=[pl.BlockSpec(out.shape, lambda i: (0, 0, 0, 0, 0))] * 2,
        out_shape=[out, out],
        scratch_shapes=[pltpu.VMEM((3, rows, HEAD), F32)],
        compiler_params=pltpu.CompilerParams(vmem_limit_bytes=24 << 20),
        cost_estimate=pl.CostEstimate(
            flops=2 * rows * width * 896, bytes_accessed=8 << 20, transcendentals=0
        ),
        name="project",
    )(x, query_weight, fresh_weight)


def attend_kernel(parts_ref, cache_ref, out_ref, sums_ref, result_ref):
    t = pl.program_id(0)

    @pl.when(t == 0)
    def _():
        total = parts_ref[0].astype(F32)
        for z in range(1, 4):
            total = total + parts_ref[z].astype(F32)
        total = total.astype(BF16).astype(F32).reshape(256, HEAD)
        for half in range(2):
            sums_ref[half] = total[:, half * 128 : half * 128 + 128]
            result_ref[half] = jnp.zeros((256, 128), F32)

    def slot(h):
        return jnp.concatenate(
            [sums_ref[half, pl.ds(h * 4 + t, 16, stride=16), :] for half in range(2)], axis=1
        )

    query = jnp.concatenate([slot(h) for h in range(3)], axis=0)
    columns = sums_ref[0, pl.ds(12 + t, 16, stride=16), :]
    fresh = [jnp.sum(columns[4 * b : 4 * b + 4], axis=0, keepdims=True) for b in range(4)]
    new_key = jnp.concatenate(fresh[:2], axis=1)
    new_value = jnp.concatenate(fresh[2:], axis=1)
    scale = HEAD ** (-0.5)
    own = jnp.sum(query * new_key, axis=1, keepdims=True) * scale
    scores = (
        lax.dot_general(
            query.astype(BF16),
            cache_ref[0, :, :HEAD],
            (((1,), (1,)), ((), ())),
            preferred_element_type=F32,
        )
        * scale
    )
    highest = jnp.maximum(jnp.max(scores, axis=1, keepdims=True), own)
    e_past = jnp.exp(scores - highest)
    e_own = jnp.exp(own - highest)
    total = jnp.sum(e_past, axis=1, keepdims=True) + e_own
    result = jnp.dot(e_past.astype(BF16), cache_ref[0, :, HEAD:], preferred_element_type=F32)
    result = (result + e_own * new_value) / total
    for h in range(3):
        for half in range(2):
            result_ref[half, pl.ds(h * 4 + t, 16, stride=16), :] = result[
                h * 16 : h * 16 + 16, half * 128 : half * 128 + 128
            ]

    @pl.when(t + lax.axis_index("c") * 4 % 4 == 3)
    def _():
        whole = jnp.concatenate([result_ref[0], result_ref[1]], axis=1)
        whole = whole.reshape(16, 16, HEAD).astype(BF16)
        for z in range(4):
            out_ref[z] = whole


def attend(parts, cache):
    return pl.pallas_call(
        attend_kernel,
        grid=(4,),
        in_specs=[
            pl.BlockSpec((4, 16, 16, HEAD), lambda t: (0, 0, 0, 0)),
            pl.BlockSpec((1,) + cache.shape[1:], lambda t: (t, 0, 0)),
        ],
        out_specs=pl.BlockSpec((4, 16, 16, HEAD), lambda t: (0, 0, 0, 0)),
        out_shape=jax.ShapeDtypeStruct((4, 16, 16, HEAD), BF16),
        scratch_shapes=[pltpu.VMEM((2, 256, 128), F32), pltpu.VMEM((2, 256, 128), F32)],
        compiler_params=pltpu.CompilerParams(vmem_limit_bytes=12 << 20),
        cost_estimate=pl.CostEstimate(
            flops=4 * 4 * 48 * 2048 * 256, bytes_accessed=10 << 20, transcendentals=1 << 19
        ),
        name="attend",
    )(parts, cache)


def output_kernel(back_ref, other_ref, weight_ref, ffn_ref, out_ref, heads_ref):
    core = lax.axis_index("c")
    z_here = lax.axis_index("z")
    tile = out_ref.shape[1]

    @pl.when(pl.program_id(0) == 0)
    def _():
        low = lower_rows((8, 8, HEAD))
        for rel, ref in ((0, back_ref), (1, other_ref)):
            for z in range(4):
                even = ref[z, :, 0].astype(F32)
                odd = ref[z, :, 1].astype(F32)
                e0, e1, o0, o1 = even[:, :8], even[:, 8:], odd[:, :8], odd[:, 8:]
                heads = [
                    jnp.where(low, e0, pltpu.roll(o0, 4, 1)),
                    jnp.where(low, pltpu.roll(e0, 4, 1), o0),
                    jnp.where(low, e1, pltpu.roll(o1, 4, 1)),
                ]
                c = core if rel == 0 else 1 - core
                rows = pl.ds(pl.multiple_of(z * 128 + c * 64, 64), 64)
                for h in range(3):
                    heads_ref[rows, h * HEAD : (h + 1) * HEAD] = heads[h].reshape(64, HEAD).astype(BF16)

    terms = jnp.dot(heads_ref[...], weight_ref[...], preferred_element_type=F32)
    for z in range(4):
        away = (z_here - z + 4) % 4
        slot = jnp.where(away == 0, 0, jnp.where(away == 1, 1, jnp.where(away == 3, 2, 3)))
        for c in range(2):
            rel = jnp.where(core == c, 0, 4)
            here = pl.ds(pl.multiple_of((rel + slot) * 64, 64), 64)
            row = z * 128 + c * 64
            out_ref[row : row + 64, :] = (terms[row : row + 64] + ffn_ref[here, :]).astype(BF16)


def output(back, other, weight, ffn):
    rows, width = ffn.shape
    tile = 768
    whole = pl.BlockSpec((4, 8, 2, 16, HEAD), lambda i: (0, 0, 0, 0, 0), pipeline_mode=pl.Buffered(1))
    return pl.pallas_call(
        output_kernel,
        grid=(width // tile,),
        in_specs=[
            whole,
            whole,
            pl.BlockSpec((weight.shape[0], tile), lambda i: (0, i)),
            pl.BlockSpec((rows, tile), lambda i: (0, i)),
        ],
        out_specs=pl.BlockSpec((rows, tile), lambda i: (0, i)),
        out_shape=jax.ShapeDtypeStruct((rows, width), BF16),
        scratch_shapes=[pltpu.VMEM((rows, weight.shape[0]), BF16)],
        compiler_params=pltpu.CompilerParams(vmem_limit_bytes=20 << 20),
        cost_estimate=pl.CostEstimate(flops=2 * rows * width * 768, bytes_accessed=12 << 20, transcendentals=0),
        name="output",
    )(back, other, weight, ffn)


def add_kernel(pieces_ref, out_ref):
    @pl.loop(0, out_ref.shape[1] // 256)
    def _(n):
        columns = pl.ds(pl.multiple_of(n * 256, 256), 256)
        total = pieces_ref[0, :, columns].astype(F32)
        for i in range(1, pieces_ref.shape[0]):
            total = total + pieces_ref[i, :, columns].astype(F32)
        out_ref[:, columns] = total.astype(BF16)


def add_pieces(pieces):
    return pl.pallas_call(
        add_kernel,
        in_specs=[pl.BlockSpec(memory_space=pltpu.VMEM)],
        out_specs=pl.BlockSpec(memory_space=pltpu.VMEM),
        out_shape=jax.ShapeDtypeStruct(pieces.shape[1:], BF16),
        compiler_params=pltpu.CompilerParams(vmem_limit_bytes=NARROW),
        name="add_pieces",
    )(pieces)


def body(residual, norm_gain, query_weight, kv_weight, cache, ffn_hidden, out_weight, down_weight):
    own_rows, width = residual.shape
    place = lax.axis_index(XY)
    rows = 16 * own_rows

    moments, kept = row_moments(residual)
    moments = moments + lax.ppermute(moments, "c", SWAP)
    moments = [moments] + [
        lax.ppermute(moments, "z", [(i, (i + k) % 4) for i in range(4)]) for k in (2, 1, 3)
    ]
    copies = normalize(kept, moments, norm_gain[None, :])
    copies, ffn_hidden, kv_weight = lax.optimization_barrier((copies, ffn_hidden, kv_weight))
    normed = lax.all_to_all(copies, XY, 0, 0).reshape(rows, width)

    hidden = [ffn_hidden] + [
        lax.ppermute(ffn_hidden, "z", [(i, (i + k) % 4) for i in range(4)]) for k in (1, 3, 2)
    ]
    ffn = feed(hidden + [lax.ppermute(v, "c", SWAP) for v in hidden], down_weight)
    columns = kv_weight.shape[1]
    mask = jnp.arange(128)[None, :] // columns == place % 4
    fresh_weight = jnp.where(mask, jnp.tile(kv_weight, (1, 128 // columns)), 0)
    normed, fresh_weight, ffn = lax.optimization_barrier((normed, fresh_weight, ffn))

    mine, theirs = project(normed, query_weight, fresh_weight)
    paired = (mine.astype(F32) + lax.ppermute(theirs, "c", SWAP).astype(F32)).astype(BF16)
    parts = lax.all_to_all(paired.reshape(64, 16, HEAD), ZXY, 0, 0)

    attended = attend(parts.reshape(4, 16, 16, HEAD), cache)
    back = lax.all_to_all(attended.reshape(64, 16, HEAD), ZXY, 0, 0).reshape(4, 8, 2, 16, HEAD)
    other = lax.ppermute(back, "c", SWAP)
    terms = output(back, other, out_weight, ffn)
    pieces = lax.all_to_all(terms.reshape(16, own_rows, width), XY, 0, 0)
    return add_pieces(pieces)


def solution(mesh):
    fine = Mesh(mesh.devices.reshape(4, 2, 4, 4), ("z", "c", "x", "y"))
    placed = (
        P(XY, ZC),
        P(ZC),
        P(ZC, XY),
        P(ZC, XY),
        P(("z", "c", "x", "y"), None, None),
        P(ZC, XY),
        P(XY, ZC),
        P(XY, ZC),
    )
    return jax.shard_map(body, mesh=fine, in_specs=placed, out_specs=P(XY, ZC), check_vma=False)
```
